128 devices in a mesh: rep: 16 (over z, y_lo, core), shard: 8 (over x, y_hi).
Axes of the slice: x: 4, y: 4 (y_hi: 2, y_lo: 2; y = y_hi * 2 + y_lo), z: 4, core: 2. Of those that a mesh axis runs over, the one named last changes fastest.
Arguments:
- tokens: bfloat16 [16384, 2048], P(('rep', 'shard')), may hold values from -6 to 6
- lengths: int32 [16], P('rep'), may hold values from 256 to 1024, as said below
- vectors: float32 [8, 2048], P(None, 'shard'), may hold values from -0.9 to 1.75
- fc1_bias: float32 [8192], P('shard'), may hold values from -1.8 to 1.8
- w_qkv: bfloat16 [2048, 6144], P('shard'), may hold values from -0.125 to 0.125
- w_dense: bfloat16 [2048, 2048], P('shard'), may hold values from -0.5 to 0.5
- w_fc1: bfloat16 [2048, 8192], P('shard'), may hold values from -0.125 to 0.125
- w_fc2: bfloat16 [8192, 2048], P('shard'), may hold values from -0.0625 to 0.0625
- cotangent: bfloat16 [16384, 2048], P(('rep', 'shard')), may hold values from -12 to 12
Outputs:
- output: bfloat16 [16384, 2048], P(('rep', 'shard'))
- d_tokens: bfloat16 [16384, 2048], P(('rep', 'shard'))
- g_vectors: float32 [8, 2048], P(None, 'shard')
- g_fc1_bias: float32 [8192], P('shard')
- g_w_qkv: float32 [2048, 6144], P('shard')
- g_w_dense: float32 [2048, 2048], P('shard')
- g_w_fc1: float32 [2048, 8192], P('shard')
- g_w_fc2: float32 [8192, 2048], P('shard')
The draws below stay inside these ranges and needn't reach their ends.
Inputs may be any that keep to these rules, and one draw needn't show every extreme that they name: `lengths`: some slot has length exactly 1024 and another exactly 256.
All inputs are finite; a program needn't handle non-finite values.
Results may differ from the reference program's by a relative error of at most 0.025.
Values may be sent and summed in bfloat16 or wider, within the bound.
No kernel may reach another device: no remote copies, remote signals or barrier semaphores. Data moves between devices by JAX's collectives and lax.ppermute only.
A program may use at most 384 MiB of HBM per device.

```python
import jax
import jax.numpy as jnp
from jax import lax

D = 2048
HEADS = 32
HEAD_DIM = 64
FF = 8192
SLOT = 1024
SLOTS = 16
TOKENS = 16384
N_SHARD = 8


def draw_lengths(key, part):
    key = jax.random.fold_in(key, 11)
    key_draw, key_order = jax.random.split(key)
    lowest = SLOT // 4
    lengths_out = jax.random.randint(key_draw, (SLOTS,), lowest, SLOT + 1)
    ranking = jax.random.permutation(key_order, SLOTS)
    lengths_out = jnp.where(ranking == 0, SLOT, lengths_out)
    lengths_out = jnp.where(ranking == 1, lowest, lengths_out)
    return lengths_out.astype(jnp.int32)


def draw_vectors(key, part):
    key = jax.random.fold_in(key, 23)
    noise = jnp.clip(jax.random.normal(key, (8, D), jnp.float32), -3.0, 3.0)
    row_index = jnp.arange(8, dtype=jnp.int32)[:, None]
    is_gain = (row_index == 0) | (row_index == 5)
    return jnp.where(is_gain, 1.0 + 0.25 * noise, 0.3 * noise).astype(jnp.float32)


def draw_cotangent(key, part):
    key = jax.random.fold_in(key, 37)
    ramp = 0.5 + 1.5 * jnp.arange(TOKENS, dtype=jnp.float32)[:, None] / TOKENS
    noise = jnp.clip(jax.random.normal(key, (TOKENS, D), jnp.float32), -6.0, 6.0)
    return (ramp * noise).astype(jnp.bfloat16)


def levels(own_key, dims, pieces, least, top_value):
    factor_of, own = 1.0, jax.random.fold_in(own_key, 6)
    for position, shards_of in pieces:
        heights = jnp.exp(jax.random.uniform(jax.random.fold_in(own, position), (shards_of,), jnp.float32, least / len(pieces), top_value / len(pieces)))
        factor_of = factor_of * jnp.repeat(heights, dims[position] // shards_of).reshape([-1 if axis == position else 1 for axis in range(len(dims))])
    return factor_of


def gaussian(rng, shape, spread, reach, cuts=(), held_as=jnp.bfloat16):
    level = levels(rng, shape, cuts, -0.22, 0.18) if cuts else 1.0
    entries = jax.random.normal(rng, shape, jnp.float32) * spread * level
    return jnp.minimum(jnp.maximum(entries, -reach), reach).astype(held_as)


def setup_inputs(seed: int = 0) -> dict:
    seeds = jax.random.split(jax.random.key(seed), 10)
    tokens = gaussian(seeds[0], (TOKENS, D), 1.0, 6.0, ((0, 128),))
    lengths = draw_lengths(jax.random.fold_in(seeds[9], 71), 0)
    vectors = draw_vectors(jax.random.fold_in(seeds[9], 71), 0)
    fc1_bias = gaussian(seeds[3], (FF,), 0.3, 1.8, ((0, 8),), jnp.float32)
    w_qkv = gaussian(seeds[4], (D, 3 * D), D ** -0.5, 0.125, ((0, 8),))
    w_dense = gaussian(seeds[5], (D, D), (D // 16) ** -0.5, 0.5, ((0, 8),))
    w_fc1 = gaussian(seeds[6], (D, FF), D ** -0.5, 0.125, ((0, 8),))
    w_fc2 = gaussian(seeds[7], (FF, D), FF ** -0.5, 0.0625, ((0, 8),))
    cotangent = draw_cotangent(jax.random.fold_in(seeds[9], 71), 0)
    return {"tokens": tokens, "lengths": lengths, "vectors": vectors, "fc1_bias": fc1_bias, "w_qkv": w_qkv, "w_dense": w_dense, "w_fc1": w_fc1, "w_fc2": w_fc2, "cotangent": cotangent}


@jax.custom_vjp
def low(v):
    return lax.optimization_barrier(v.astype(jnp.bfloat16)).astype(jnp.float32)

@jax.custom_vjp
def low_back(v):
    return v

def low_keep(v):
    return (low(v), None)

def low_pass(kept, grad):
    return (grad,)

def back_keep(v):
    return (v, None)

def back_low(kept, grad):
    return (low(grad),)
low.defvjp(low_keep, low_pass)
low_back.defvjp(back_keep, back_low)
epsilon = 1e-05
highest = lax.Precision.HIGHEST

def rounded_both(values):
    return low(low_back(values))

def matmul(left, right):
    return jnp.dot(left, right, precision=highest, preferred_element_type=jnp.float32)

def layer_norm(values, gain_row, shift_row):
    average = lax.optimization_barrier(jnp.mean(values, axis=-1, keepdims=True))
    centred = values - average
    variance = lax.optimization_barrier(jnp.mean(centred * centred, axis=-1, keepdims=True))
    return centred * lax.rsqrt(variance + epsilon) * gain_row + shift_row

def attend(queries, key_rows, value_rows, positions):
    query_heads = queries.reshape(SLOT, HEADS, HEAD_DIM)
    key_heads = key_rows.reshape(SLOT, HEADS, HEAD_DIM)
    value_heads = value_rows.reshape(SLOT, HEADS, HEAD_DIM)
    raw = jnp.einsum('qhd,khd->hqk', query_heads, key_heads, precision=highest)
    distance = (positions[None, :] - positions[:, None]).astype(jnp.float32)
    slopes = jnp.exp2(-8.0 * (jnp.arange(HEADS, dtype=jnp.float32) + 1.0) / HEADS)
    scores = low_back(raw * HEAD_DIM ** (-0.5) + slopes[:, None, None] * distance[None])
    causal = positions[None, :] <= positions[:, None]
    masked = jnp.where(causal[None], scores, -1e+30)
    attention = jax.nn.softmax(masked, axis=-1)
    context = jnp.einsum('hqk,khd->qhd', low(attention), value_heads, precision=highest)
    return context.reshape(SLOT, D)

def forward(tokens_in, vectors, fc1_bias, w_qkv, w_dense, w_fc1, w_fc2, valid_rows, positions):
    normed = layer_norm(tokens_in, vectors[0], vectors[1])
    projected = matmul(low(normed), w_qkv)
    queries = rounded_both(projected[:, :D] + vectors[2])
    key_rows = rounded_both(projected[:, D:2 * D])
    value_rows = rounded_both(projected[:, 2 * D:] + vectors[3])
    context = attend(queries, key_rows, value_rows, positions)
    attn_out = low_back(matmul(rounded_both(context), w_dense) + vectors[4])
    hidden = tokens_in + attn_out
    normed_two = layer_norm(hidden, vectors[5], vectors[6])
    pre_act = low_back(matmul(low(normed_two), w_fc1) + fc1_bias)
    activated = rounded_both(jax.nn.gelu(pre_act, approximate=False))
    mlp_out = matmul(activated, w_fc2) + vectors[7]
    return valid_rows[:, None] * (hidden + mlp_out)

def reference(tokens, lengths, vectors, fc1_bias, w_qkv, w_dense, w_fc1, w_fc2, cotangent):
    shard_rows = SLOT // N_SHARD
    positions = jnp.arange(SLOT, dtype=jnp.int32)
    params = (vectors.astype(jnp.float32), fc1_bias.astype(jnp.float32), w_qkv.astype(jnp.float32), w_dense.astype(jnp.float32), w_fc1.astype(jnp.float32), w_fc2.astype(jnp.float32))

    def reorder(block):
        return block.reshape(N_SHARD, shard_rows, D).transpose(1, 0, 2).reshape(SLOT, D)

    def restore(block):
        return block.reshape(shard_rows, N_SHARD, D).transpose(1, 0, 2).reshape(SLOT, D)

    def one_slot(totals, inputs):
        slot_tokens, slot_cot, length = inputs
        valid_rows = (positions < length).astype(jnp.float32)

        def layer_run(tokens_in, vec_in, bias_in, qkv_in, dense_in, fc1_in, fc2_in):
            return forward(tokens_in, vec_in, bias_in, qkv_in, dense_in, fc1_in, fc2_in, valid_rows, positions)
        result, pullback = jax.vjp(layer_run, reorder(slot_tokens.astype(jnp.float32)), *params)
        gradients = pullback(reorder(slot_cot.astype(jnp.float32)))
        new_totals = tuple((first_sum + second_sum for first_sum, second_sum in zip(totals, gradients[1:])))
        return (new_totals, (restore(result).astype(jnp.bfloat16), restore(gradients[0]).astype(jnp.bfloat16)))
    zero_sums = tuple((jnp.zeros_like(param) for param in params))
    totals, (outputs, input_grads) = lax.scan(one_slot, zero_sums, (tokens.reshape(SLOTS, SLOT, D), cotangent.reshape(SLOTS, SLOT, D), lengths))
    return (outputs.reshape(TOKENS, D), input_grads.reshape(TOKENS, D), totals[0], totals[1], totals[2], totals[3], totals[4], totals[5])
```

```python
import numpy as np
import jax
import jax.numpy as jnp
from jax import lax
from jax.sharding import Mesh
from jax.sharding import PartitionSpec as P

HEAD_DIM = 64
EPSILON = 1e-05
bf16 = jnp.bfloat16
f32 = jnp.float32

ALL = ("z", "yl", "c", "x", "yh")
NX, NZ = 4, 4
SWAP = [(0, 0), (1, 2), (2, 1), (3, 3)]


def move(values):
    return lax.ppermute(values, ("c", "yh"), SWAP)


def across_core(values):
    return lax.ppermute(values, "c", [(0, 1), (1, 0)])


def along_x(values, step):
    return lax.ppermute(values, "x", [(i, (i + step) % NX) for i in range(NX)])


def along_z(values, step):
    return lax.ppermute(values, "z", [(i, (i + step) % NZ) for i in range(NZ)])


def gather_rows(block):
    other = across_core(block)
    mine = [along_x(block, k) for k in (1, 3, 2)]
    theirs = across_core(jnp.stack(mine))
    return jnp.stack(
        [
            jnp.stack([block, other]),
            jnp.stack([mine[0], theirs[0]]),
            jnp.stack([mine[2], theirs[2]]),
            jnp.stack([mine[1], theirs[1]]),
        ]
    )


def scatter_rows(parts):
    sent = across_core(parts[:, 1].astype(bf16))
    chip = parts[:, 0] + sent.astype(f32)
    got = [along_x(chip[k].astype(bf16), -k) for k in (2, 1, 3)]
    return chip[0] + got[0].astype(f32) + got[1].astype(f32) + got[2].astype(f32)


def normalize(values):
    average = jnp.mean(values, axis=-1, keepdims=True)
    centred = values - average
    variance = jnp.mean(centred * centred, axis=-1, keepdims=True)
    inverse = lax.rsqrt(variance + EPSILON)
    return centred * inverse, inverse


def norm_back(grad_out, normed, inverse, gain_row):
    scaled = grad_out * gain_row
    inner = (
        scaled
        - jnp.mean(scaled, axis=-1, keepdims=True)
        - normed * jnp.mean(scaled * normed, axis=-1, keepdims=True)
    )
    return inner * inverse


def dot(left, right):
    return jnp.dot(left, right, preferred_element_type=f32)


def dot_t(left, right):
    return lax.dot_general(left, right, (((1,), (1,)), ((), ())), preferred_element_type=f32)


def t_dot(left, right):
    return lax.dot_general(left, right, (((0,), (0,)), ((), ())), preferred_element_type=f32)


def local(tokens, lengths, vectors, fc1_bias, w_qkv, w_dense, w_fc1, w_fc2, cotangent):
    rows, width = tokens.shape
    ax, az = lax.axis_index("x"), lax.axis_index("z")
    core, yh = lax.axis_index("c"), lax.axis_index("yh")
    part = width // 8
    ff_part = fc1_bias.shape[0]
    heads = part // HEAD_DIM
    slot = rows * 8
    scale = HEAD_DIM ** (-0.5)
    own_pos = jnp.arange(rows, dtype=jnp.int32) * 8 + ax * 2 + yh
    valid = (own_pos < lengths[0]).astype(f32)[:, None]

    tok = move(tokens)
    dm_own = move((valid * cotangent.astype(f32)).astype(bf16))
    x_all = gather_rows(tok).reshape(slot, width)

    sub = w_qkv.shape[0] // NZ

    def piece_for(step):
        member = ((ax + step) % NX) * 2 + core
        row = az * sub
        cols = [
            lax.dynamic_slice(w_qkv, (row, i * width + member * part), (sub, part)) for i in range(3)
        ]
        cols.append(lax.dynamic_slice(w_fc1, (row, member * ff_part), (sub, ff_part)))
        return jnp.concatenate(cols, 1)

    pieces = [piece_for(0)] + [along_x(piece_for(k), k) for k in (1, 2, 3)]
    by_x = jnp.zeros((NX,) + pieces[0].shape, bf16)
    for k in range(NX):
        by_x = lax.dynamic_update_slice(by_x, pieces[k][None], ((ax - k) % NX, 0, 0))
    from_y = lax.ppermute(by_x, ("yl", "yh"), [(0, 3), (1, 2), (2, 1), (3, 0)])
    by_xy = jnp.where(yh == 0, jnp.stack([by_x, from_y], 1), jnp.stack([from_y, by_x], 1))

    def over_z(block):
        cols = block.shape[-1]
        block = block.reshape(8, 1, sub, cols)
        full = jnp.zeros((8, NZ, sub, cols), bf16)
        for k in range(NZ):
            got = block if k == 0 else along_z(block, k)
            full = lax.dynamic_update_slice(full, got, (0, (az - k) % NZ, 0, 0))
        return full.reshape(width, cols)

    wq = over_z(by_xy[..., : 3 * part])
    wf1 = over_z(by_xy[..., 3 * part :])
    wd = move(w_dense)
    wf2 = move(w_fc2)
    vec_all = lax.all_gather(vectors, ("x", "yh"), axis=1, tiled=True)
    vec_part = move(vectors)
    bias_part = move(fc1_bias)

    inputs = x_all.astype(f32)
    unit_one, _ = normalize(inputs)
    a_b = (unit_one * vec_all[0] + vec_all[1]).astype(bf16)
    projected = dot(a_b, wq)
    query = (projected[:, :part] + vec_part[2]).astype(bf16)
    key = projected[:, part : 2 * part].astype(bf16)
    value = (projected[:, 2 * part :] + vec_part[3]).astype(bf16)

    steps = jnp.arange(4, dtype=jnp.int32)[:, None, None]
    others = jnp.arange(2, dtype=jnp.int32)[None, :, None]
    member = ((ax - steps) % NX) * 2 + (core ^ others)
    pos = (jnp.arange(rows, dtype=jnp.int32)[None, None, :] * 8 + member).reshape(slot)
    head = ((ax * 2 + core) * heads + jnp.arange(heads, dtype=jnp.int32)).astype(f32)
    slopes = jnp.exp2(-8.0 * (head + 1.0) / (heads * 8))
    distance = (pos[None, :] - pos[:, None]).astype(f32)
    causal = (pos[None, :] <= pos[:, None])[None]
    qh = query.reshape(slot, heads, HEAD_DIM)
    kh = key.reshape(slot, heads, HEAD_DIM)
    vh = value.reshape(slot, heads, HEAD_DIM)

    def scores():
        raw = jnp.einsum("qhd,khd->hqk", qh, kh, preferred_element_type=f32)
        return jnp.where(causal, raw * scale + slopes[:, None, None] * distance[None], -1e30)

    s = scores()
    row_max = jnp.max(s, axis=-1, keepdims=True)
    exponent = jnp.exp(s - row_max)
    total = jnp.sum(exponent, axis=-1, keepdims=True)
    lse = row_max + jnp.log(total)
    att_b = (exponent / total).astype(bf16)
    ctx_b = (
        jnp.einsum("hqk,khd->qhd", att_b, vh, preferred_element_type=f32)
        .reshape(slot, part)
        .astype(bf16)
    )
    hidden = (
        tok.astype(f32)
        + scatter_rows(dot(ctx_b, wd).reshape(4, 2, rows, width))
        + vec_all[4]
    )
    unit_two, inverse_two = normalize(hidden)
    c_own = (unit_two * vec_all[5] + vec_all[6]).astype(bf16)
    c_b = gather_rows(c_own).reshape(slot, width)
    dm = gather_rows(dm_own).reshape(slot, width)
    pre = dot(c_b, wf1) + bias_part
    activated, gelu_back = jax.vjp(lambda v: jax.nn.gelu(v, approximate=False), pre)
    act_b = activated.astype(bf16)
    d_act = dot_t(dm, wf2).astype(bf16)
    du_b = gelu_back(d_act.astype(f32))[0].astype(bf16)
    dc = scatter_rows(dot_t(du_b, wf1).reshape(4, 2, rows, width))
    out_own = hidden + scatter_rows(dot(act_b, wf2).reshape(4, 2, rows, width)) + vec_all[7]
    output = (valid * move(out_own.astype(bf16)).astype(f32)).astype(bf16)
    g_fc2 = t_dot(act_b, dm).astype(bf16)
    g_fc1 = t_dot(c_b, du_b).astype(bf16)
    dh = dm_own.astype(f32) + norm_back(dc, unit_two, inverse_two, vec_all[5])
    dh_own = dh.astype(bf16)
    dh_b = gather_rows(dh_own).reshape(slot, width)
    g_dense = t_dot(ctx_b, dh_b).astype(bf16)
    dctx = dot_t(dh_b, wd).astype(bf16).reshape(slot, heads, HEAD_DIM)

    att = jnp.exp(scores() - lse)
    d_prob = jnp.einsum("qhd,khd->hqk", dctx, vh, preferred_element_type=f32)
    inner = jnp.sum(att * d_prob, axis=-1, keepdims=True)
    ds_b = (att * (d_prob - inner)).astype(bf16)
    dq = jnp.einsum("hqk,khd->qhd", ds_b, kh, preferred_element_type=f32) * scale
    dk = jnp.einsum("hqk,qhd->khd", ds_b, qh, preferred_element_type=f32) * scale
    dv = jnp.einsum("hqk,qhd->khd", att.astype(bf16), dctx, preferred_element_type=f32)
    d_proj = jnp.concatenate([t.reshape(slot, part).astype(bf16) for t in (dq, dk, dv)], 1)
    g_qkv = t_dot(a_b, d_proj).astype(bf16)
    da = scatter_rows(dot_t(d_proj, wq).reshape(4, 2, rows, width))
    own_unit, own_inverse = normalize(tok.astype(f32))
    d_tokens = move((dh + norm_back(da, own_unit, own_inverse, vec_all[0])).astype(bf16))

    slots = ("z", "yl", "yh")
    home = yh == core

    def summed(values):
        return lax.psum(values.astype(bf16), slots)

    def rows_home(values):
        return jnp.where(home, values, across_core(values)).astype(f32)

    def columns_home(values, groups):
        cols = values.shape[1]
        mine = lax.dynamic_slice(
            values.reshape(NX, 2, part, cols), (0, yh, 0, 0), (NX, 1, part, cols)
        ).reshape(NX, part, cols)
        by_source = jnp.zeros((NX, part, cols), bf16)
        for k in range(NX):
            block = lax.dynamic_slice(mine, ((ax + k) % NX, 0, 0), (1, part, cols))
            got = block if k == 0 else along_x(block, k)
            by_source = lax.dynamic_update_slice(by_source, got, ((ax - k) % NX, 0, 0))
        theirs = across_core(by_source)
        both = jnp.where(
            core == 0, jnp.stack([by_source, theirs], 1), jnp.stack([theirs, by_source], 1)
        )
        return (
            both.reshape(8, part, groups, cols // groups)
            .transpose(1, 2, 0, 3)
            .reshape(part, 8 * cols)
            .astype(f32)
        )

    grad_fc2 = rows_home(summed(g_fc2))
    grad_fc1 = columns_home(summed(g_fc1), 1)
    grad_dense = rows_home(summed(g_dense))
    grad_qkv = columns_home(summed(g_qkv), 3)
    token_terms = jnp.stack(
        [
            jnp.sum(da * own_unit, 0),
            jnp.sum(da, 0),
            jnp.sum(dh_own.astype(f32), 0),
            jnp.sum(dc * unit_two, 0),
            jnp.sum(dc, 0),
            jnp.sum(dm_own.astype(f32), 0),
        ]
    )
    token_terms = lax.psum(token_terms.astype(bf16), ALL).astype(f32)
    token_terms = lax.dynamic_slice(token_terms, (0, (ax * 2 + yh) * part), (6, part))
    member_terms = jnp.concatenate(
        [
            jnp.sum(d_proj[:, :part].astype(f32), 0),
            jnp.sum(d_proj[:, 2 * part :].astype(f32), 0),
            jnp.sum(du_b.astype(f32), 0),
        ]
    )
    member_terms = rows_home(summed(member_terms))
    grad_vectors = jnp.concatenate(
        [token_terms[:2], member_terms[: 2 * part].reshape(2, part), token_terms[2:]]
    )
    return (
        output,
        d_tokens,
        grad_vectors,
        member_terms[2 * part :],
        grad_qkv,
        grad_dense,
        grad_fc1,
        grad_fc2,
    )


def solution(mesh):
    fine = Mesh(np.asarray(mesh.devices).reshape(4, 2, 2, 4, 2), ALL)
    rows = P(("z", "yl", "c", "x", "yh"), None)
    shard = P(("x", "yh"), None)
    return jax.shard_map(
        local,
        mesh=fine,
        in_specs=(
            rows,
            P(("z", "yl", "c")),
            P(None, ("x", "yh")),
            P(("x", "yh")),
            shard,
            shard,
            shard,
            shard,
            rows,
        ),
        out_specs=(
            rows,
            rows,
            P(None, ("x", "yh")),
            P(("x", "yh")),
            shard,
            shard,
            shard,
            shard,
        ),
        check_vma=False,
    )
```

```python
import functools

import numpy as np
import jax
import jax.numpy as jnp
from jax import lax
from jax.experimental import pallas as pl
from jax.experimental.pallas import tpu as pltpu
from jax.sharding import Mesh
from jax.sharding import PartitionSpec as P

HEAD_DIM = 64
EPSILON = 1e-05
bf16 = jnp.bfloat16
f32 = jnp.float32

ALL = ("z", "yl", "c", "x", "yh")
NX, NZ = 4, 4
SWAP = [(1, 2), (2, 1)]


def move(values):
    got = lax.ppermute(values, ("c", "yh"), SWAP)
    return jnp.where(lax.axis_index("c") == lax.axis_index("yh"), values, got)


def move_late(values, after):
    got = gate([lax.ppermute(values, ("c", "yh"), SWAP)], after)[0]
    return jnp.where(lax.axis_index("c") == lax.axis_index("yh"), values, got)


def across_core(values):
    return lax.ppermute(values, "c", [(0, 1), (1, 0)])


def along_x(values, step):
    return lax.ppermute(values, "x", [(i, (i + step) % NX) for i in range(NX)])


def along_z(values, step):
    return lax.ppermute(values, "z", [(i, (i + step) % NZ) for i in range(NZ)])


def along_y(values, flip_yl, flip_yh):
    pairs = [(i, i ^ (2 * flip_yl + flip_yh)) for i in range(4)]
    return lax.ppermute(values, ("yl", "yh"), pairs)


def gather_rows(block):
    mine = {0: block}
    for k in (1, 3, 2):
        mine[k] = along_x(block, k)
    theirs = {k: across_core(mine[k]) for k in (0, 1, 3, 2)}
    return [part[k] for k in range(NX) for part in (mine, theirs)]


def where_blocks():
    ax, core = lax.axis_index("x"), lax.axis_index("c")
    return jnp.stack(
        [(core ^ r) * NX + (ax - k) % NX for k in range(NX) for r in range(2)]
    ).astype(jnp.int32)


def gate(values, after):
    anywhere = pl.BlockSpec(memory_space=pl.ANY)
    out = pl.pallas_call(
        lambda *refs: None,
        in_specs=[anywhere] * (len(values) + len(after)),
        out_specs=[anywhere] * len(values),
        out_shape=[jax.ShapeDtypeStruct(v.shape, v.dtype) for v in values],
        input_output_aliases={i: i for i in range(len(values))},
        cost_estimate=cost(0),
        name="gate",
    )(*values, *after)
    return list(out)


def cost(us):
    return pl.CostEstimate(flops=int(us * 1e9), bytes_accessed=int(us * 3.2e6), transcendentals=0)


def kernel_params(mib=56):
    return pltpu.CompilerParams(vmem_limit_bytes=mib << 20)


def theirs_kernel(info_ref, left_ref, right_ref, out_ref, *, contract):
    rows = left_ref.shape[1]
    out_ref[...] = lax.dot_general(
        left_ref[...].reshape(NX * rows, left_ref.shape[2]),
        right_ref[...],
        contract,
        preferred_element_type=f32,
    ).astype(out_ref.dtype)


def mine_kernel(info_ref, left_ref, right_ref, got_ref, *refs, contract):
    outs, sum_ref = refs[:NX], refs[NX]
    rows = left_ref.shape[1]
    sum_ref[...] = lax.dot_general(
        left_ref[...].reshape(NX * rows, left_ref.shape[2]),
        right_ref[...],
        contract,
        preferred_element_type=f32,
    ) + got_ref[...].astype(f32)
    for k in range(NX):
        at = pl.ds(pl.multiple_of(info_ref[1 + k] * rows, rows), rows)
        outs[k][...] = sum_ref[at, :].astype(outs[k].dtype)


def group_info():
    ax, core = lax.axis_index("x"), lax.axis_index("c")
    return jnp.stack([core] + [(ax - k) % NX for k in range(NX)]).astype(jnp.int32)


def right_side(right, transposed, tile):
    if transposed:
        return right.shape[0], pl.BlockSpec((tile, right.shape[1]), lambda n, info: (n, 0))
    return right.shape[1], pl.BlockSpec((right.shape[0], tile), lambda n, info: (0, n))


def theirs_part(left, right, transposed, name, tile=512):
    rows, depth = left.shape[1:]
    width, right_spec = right_side(right, transposed, tile)
    contract = (((1,), (1 if transposed else 0,)), ((), ()))
    sent = pl.pallas_call(
        functools.partial(theirs_kernel, contract=contract),
        grid_spec=pltpu.PrefetchScalarGridSpec(
            num_scalar_prefetch=1,
            grid=(width // tile,),
            in_specs=[
                pl.BlockSpec((NX, rows, depth), lambda n, info: (1 - info[0], 0, 0)),
                right_spec,
            ],
            out_specs=pl.BlockSpec((NX * rows, tile), lambda n, info: (0, n)),
        ),
        out_shape=jax.ShapeDtypeStruct((NX * rows, width), bf16),
        compiler_params=kernel_params(),
        cost_estimate=cost(5.0 if depth < 512 else 6.5),
        name=name + "_theirs",
    )(group_info(), left, right)
    return across_core(sent)


def mine_part(left, right, got, transposed, name, tile=512):
    rows, depth = left.shape[1:]
    width, right_spec = right_side(right, transposed, tile)
    contract = (((1,), (1 if transposed else 0,)), ((), ()))
    return pl.pallas_call(
        functools.partial(mine_kernel, contract=contract),
        grid_spec=pltpu.PrefetchScalarGridSpec(
            num_scalar_prefetch=1,
            grid=(width // tile,),
            in_specs=[
                pl.BlockSpec((NX, rows, depth), lambda n, info: (info[0], 0, 0)),
                right_spec,
                pl.BlockSpec((NX * rows, tile), lambda n, info: (0, n)),
            ],
            out_specs=[pl.BlockSpec((rows, tile), lambda n, info: (0, n))] * NX,
            scratch_shapes=[pltpu.VMEM((NX * rows, tile), f32)],
        ),
        out_shape=[jax.ShapeDtypeStruct((rows, width), f32 if k == 0 else bf16) for k in range(NX)],
        compiler_params=kernel_params(),
        cost_estimate=cost(5.4 if depth < 512 else 7.0),
        name=name + "_mine",
    )(group_info(), left, right, got)


def send_chips(chips):
    return [chips[0]] + [along_x(chips[k], -k) for k in (2, 1, 3)]


def scatter_rows(left, right, transposed, name):
    got = theirs_part(left, right, transposed, name)
    return send_chips(mine_part(left, right, got, transposed, name))


def total(terms):
    result = terms[0]
    for term in terms[1:]:
        result = result + term.astype(f32)
    return result


def row_call(kernel, blocks, fixed, per_row, outs, name, us):
    whole = lambda v: pl.BlockSpec(v.shape, lambda i, at, nd=len(v.shape): (0,) * nd)
    return pl.pallas_call(
        kernel,
        grid_spec=pltpu.PrefetchScalarGridSpec(
            num_scalar_prefetch=1,
            grid=(1,),
            in_specs=[whole(v) for v in blocks + fixed + per_row],
            out_specs=[whole(v) for v in outs],
        ),
        out_shape=outs,
        compiler_params=kernel_params(),
        cost_estimate=cost(us),
        name=name,
    )(where_blocks(), *blocks, *fixed, *per_row)


def collect_kernel(at_ref, *refs):
    for i in range(8):
        refs[8][at_ref[i]] = refs[i][...]


def pair_of(refs, k):
    return jnp.concatenate([refs[2 * k][...], refs[2 * k + 1][...]], 0)


def put_pair(ref, at_ref, k, values):
    rows = ref.shape[1]
    for r in range(2):
        ref[at_ref[2 * k + r]] = values[r * rows : (r + 1) * rows]


def norm_kernel(at_ref, *refs):
    blocks, (gain_ref, a_ref) = refs[:8], refs[8:]
    for i in range(8):
        unit, _ = normalize(blocks[i][...].astype(f32))
        a_ref[at_ref[i]] = (unit * gain_ref[0:1, :] + gain_ref[1:2, :]).astype(bf16)


def qkv_kernel(a_ref, weight_ref, bias_ref, qkv_ref):
    blocks, rows, depth = a_ref.shape
    out = jnp.dot(
        a_ref[...].reshape(blocks * rows, depth), weight_ref[...], preferred_element_type=f32
    )
    qkv_ref[...] = (out + bias_ref[...]).astype(bf16).reshape(blocks, rows, out.shape[1])


def project_qkv(a_b, weight, bias):
    blocks, rows, depth = a_b.shape
    cols, step = weight.shape[1], 2
    return pl.pallas_call(
        qkv_kernel,
        grid=(blocks // step,),
        in_specs=[
            pl.BlockSpec((step, rows, depth), lambda i: (i, 0, 0)),
            pl.BlockSpec(weight.shape, lambda i: (0, 0)),
            pl.BlockSpec(bias.shape, lambda i: (0, 0)),
        ],
        out_specs=pl.BlockSpec((step, rows, cols), lambda i: (i, 0, 0)),
        out_shape=jax.ShapeDtypeStruct((blocks, rows, cols), bf16),
        compiler_params=kernel_params(),
        cost_estimate=cost(7.0),
        name="qkv",
    )(a_b, weight, bias)


def mlp_kernel(at_ref, *refs):
    blocks, (weight_ref, bias_ref, d_act_ref, c_ref, act_ref, du_ref, sum_ref) = refs[:8], refs[8:]
    sums = jnp.zeros(sum_ref.shape, f32)
    for k in range(NX):
        c = pair_of(blocks, k)
        put_pair(c_ref, at_ref, k, c)
        pre = jnp.dot(c, weight_ref[...], preferred_element_type=f32) + bias_ref[...]
        share = 0.5 + 0.5 * lax.erf(pre * (0.5**0.5))
        put_pair(act_ref, at_ref, k, (pre * share).astype(bf16))
        slope = share + pre * (jnp.exp(-0.5 * pre * pre) * ((2.0 * np.pi) ** -0.5))
        d_act = jnp.concatenate([d_act_ref[at_ref[2 * k]], d_act_ref[at_ref[2 * k + 1]]], 0)
        du = (d_act.astype(f32) * slope).astype(bf16)
        put_pair(du_ref, at_ref, k, du)
        sums = sums + jnp.sum(du.astype(f32), axis=0, keepdims=True)
    sum_ref[...] = sums


def ctx_back_kernel(at_ref, *refs):
    blocks, (weight_ref, dh_ref, out_ref) = refs[:8], refs[8:]
    for k in range(NX):
        dh = pair_of(blocks, k)
        put_pair(dh_ref, at_ref, k, dh)
        out = lax.dot_general(
            dh, weight_ref[...], (((1,), (1,)), ((), ())), preferred_element_type=f32
        )
        put_pair(out_ref, at_ref, k, out.astype(bf16))


def normalize(values):
    average = jnp.mean(values, axis=-1, keepdims=True)
    centred = values - average
    variance = jnp.mean(centred * centred, axis=-1, keepdims=True)
    inverse = lax.rsqrt(variance + EPSILON)
    return centred * inverse, inverse


def norm_back(grad_out, normed, inverse, gain_row):
    scaled = grad_out * gain_row
    inner = (
        scaled
        - jnp.mean(scaled, axis=-1, keepdims=True)
        - normed * jnp.mean(scaled * normed, axis=-1, keepdims=True)
    )
    return inner * inverse


def dot(left, right):
    return jnp.dot(left, right, preferred_element_type=f32)


def dot_t(left, right):
    return lax.dot_general(left, right, (((1,), (1,)), ((), ())), preferred_element_type=f32)


def t_dot(left, right):
    return lax.dot_general(left, right, (((0,), (0,)), ((), ())), preferred_element_type=f32)


TB = 32
MASKED = -1e30


def first_position(block):
    return block % NX * 2 + block // NX


def attention_setup(slope_ref, bias_ref, pos_ref, head):
    blocks, rows, lanes = pos_ref.shape
    slope = slope_ref[head]
    steps = lax.broadcasted_iota(jnp.int32, (rows, lanes), 0).astype(f32) * 8.0
    for block in range(blocks):
        at = steps + float(first_position(block))
        pos_ref[block] = at
        bias_ref[block] = at * slope
    return slope


def query_positions(start):
    lane = lax.broadcasted_iota(jnp.int32, (1, 8 * TB), 1)
    block, step = lane // TB, lane % TB
    return ((start + step) * 8 + first_position(block)).astype(f32)


def masked_scores(keys, queries, bias_ref, pos_ref, slope, i):
    count = 8 * TB * (i + 1)
    raw = lax.dot_general(
        keys, queries, (((1,), (1,)), ((), ())), preferred_element_type=f32
    )
    offset = slope * float(8 * TB * i)
    half = bias_ref.shape[2]
    bias = bias_ref[:, : TB * (i + 1), :].reshape(count, half) - offset
    pos = pos_ref[:, : TB * (i + 1), :].reshape(count, half)
    at = query_positions(TB * i)
    parts = [
        jnp.where(
            pos <= at[:, side * half : (side + 1) * half],
            raw[:, side * half : (side + 1) * half] + bias,
            MASKED,
        )
        for side in range(2)
    ]
    return jnp.concatenate(parts, 1)


def block_rows(ref, start, stop):
    return ref[:, start:stop, :].reshape(8 * (stop - start), ref.shape[2])


def attention_kernel(slope_ref, q_ref, k_ref, v_ref, ctx_ref, lse_ref, bias_ref, pos_ref):
    pair, side = pl.program_id(0), pl.program_id(1)
    slope = attention_setup(slope_ref, bias_ref, pos_ref, pair * 2 + side)
    lanes = lax.broadcasted_iota(jnp.int32, (1, 2 * HEAD_DIM), 1) // HEAD_DIM
    mine = lanes == side
    pick = mine.astype(bf16)
    for i in range(q_ref.shape[1] // TB):
        queries = block_rows(q_ref, TB * i, TB * (i + 1)) * (pick * (HEAD_DIM**-0.5))
        keys = block_rows(k_ref, 0, TB * (i + 1))
        values = block_rows(v_ref, 0, TB * (i + 1))
        s = masked_scores(keys, queries, bias_ref, pos_ref, slope, i)
        top = jnp.max(s, axis=0, keepdims=True)
        e = jnp.exp(s - top)
        total = jnp.sum(e, axis=0, keepdims=True)
        att = (e * (1.0 / total)).astype(bf16)
        ctx = lax.dot_general(
            values, att, (((0,), (0,)), ((), ())), preferred_element_type=f32
        ).T.reshape(8, TB, 2 * HEAD_DIM)
        before = ctx_ref[:, TB * i : TB * (i + 1), :]
        ctx_ref[:, TB * i : TB * (i + 1), :] = jnp.where(
            mine[:, None, :], ctx.astype(bf16), before
        )
        lse_ref[0, i : i + 1, :] = top + jnp.log(total)


def attention_back_kernel(
    slope_ref, q_ref, k_ref, v_ref, do_ref, lse_ref, out_ref, bias_ref, pos_ref, dk_ref, dv_ref
):
    pair, side = pl.program_id(0), pl.program_id(1)
    slope = attention_setup(slope_ref, bias_ref, pos_ref, pair * 2 + side)
    lanes = lax.broadcasted_iota(jnp.int32, (1, 2 * HEAD_DIM), 1) // HEAD_DIM
    mine = lanes == side
    pick = mine.astype(bf16)
    scale = HEAD_DIM**-0.5
    width = 2 * HEAD_DIM

    @pl.when(side == 0)
    def _():
        dk_ref[...] = jnp.zeros_like(dk_ref)
        dv_ref[...] = jnp.zeros_like(dv_ref)

    at_q = pl.ds(pl.multiple_of(pair * width, width), width)
    for i in range(q_ref.shape[1] // TB):
        queries = block_rows(q_ref, TB * i, TB * (i + 1)) * (pick * scale)
        grads = block_rows(do_ref, TB * i, TB * (i + 1)) * pick
        keys = block_rows(k_ref, 0, TB * (i + 1))
        values = block_rows(v_ref, 0, TB * (i + 1))
        s = masked_scores(keys, queries, bias_ref, pos_ref, slope, i)
        att = jnp.exp(s - lse_ref[0, i : i + 1, :])
        d_prob = lax.dot_general(
            values, grads, (((1,), (1,)), ((), ())), preferred_element_type=f32
        )
        inner = jnp.sum(att * d_prob, axis=0, keepdims=True)
        ds = (att * (d_prob - inner)).astype(bf16)
        shape = (8, TB * (i + 1), width)
        dv_ref[:, : TB * (i + 1), :] += jnp.dot(
            att.astype(bf16), grads, preferred_element_type=f32
        ).reshape(shape)
        dk_ref[:, : TB * (i + 1), :] += jnp.dot(
            ds, queries, preferred_element_type=f32
        ).reshape(shape)
        dq = lax.dot_general(
            keys, ds, (((0,), (0,)), ((), ())), preferred_element_type=f32
        ).T.reshape(8, TB, width)
        before = out_ref[:, TB * i : TB * (i + 1), at_q]
        out_ref[:, TB * i : TB * (i + 1), at_q] = jnp.where(
            mine[:, None, :], (dq * scale).astype(bf16), before
        )

    @pl.when(side == 1)
    def _():
        part = out_ref.shape[2] // 3
        at_k = pl.ds(pl.multiple_of(part + pair * width, width), width)
        at_v = pl.ds(pl.multiple_of(2 * part + pair * width, width), width)
        out_ref[:, :, at_k] = dk_ref[...].astype(bf16)
        out_ref[:, :, at_v] = dv_ref[...].astype(bf16)


def qkv_specs(rows, pairs):
    width = 2 * HEAD_DIM
    return [
        pl.BlockSpec((8, rows, width), lambda g, h, *_, first=first: (0, 0, first + g))
        for first in (0, pairs, 2 * pairs)
    ]


def attention(qkv, slopes):
    rows, part = qkv.shape[1], qkv.shape[2] // 3
    pairs, width = part // (2 * HEAD_DIM), 2 * HEAD_DIM
    return pl.pallas_call(
        attention_kernel,
        grid_spec=pltpu.PrefetchScalarGridSpec(
            num_scalar_prefetch=1,
            grid=(pairs, 2),
            in_specs=qkv_specs(rows, pairs),
            out_specs=[
                pl.BlockSpec((8, rows, width), lambda g, h, *_: (0, 0, g)),
                pl.BlockSpec((1, rows // TB, 8 * TB), lambda g, h, *_: (2 * g + h, 0, 0)),
            ],
            scratch_shapes=[
                pltpu.VMEM((8, rows, width), f32),
                pltpu.VMEM((8, rows, width), f32),
            ],
        ),
        out_shape=[
            jax.ShapeDtypeStruct((8, rows, part), bf16),
            jax.ShapeDtypeStruct((2 * pairs, rows // TB, 8 * TB), f32),
        ],
        compiler_params=pltpu.CompilerParams(vmem_limit_bytes=40 << 20),
        cost_estimate=cost(10.2),
        name="attention",
    )(slopes, qkv, qkv, qkv)


def attention_back(qkv, d_ctx, lse, slopes):
    rows, part = qkv.shape[1], qkv.shape[2] // 3
    pairs, width = part // (2 * HEAD_DIM), 2 * HEAD_DIM
    return pl.pallas_call(
        attention_back_kernel,
        grid_spec=pltpu.PrefetchScalarGridSpec(
            num_scalar_prefetch=1,
            grid=(pairs, 2),
            in_specs=qkv_specs(rows, pairs)
            + [
                pl.BlockSpec((8, rows, width), lambda g, h, *_: (0, 0, g)),
                pl.BlockSpec((1, rows // TB, 8 * TB), lambda g, h, *_: (2 * g + h, 0, 0)),
            ],
            out_specs=pl.BlockSpec((8, rows, 3 * part), lambda g, h, *_: (0, 0, 0)),
            scratch_shapes=[pltpu.VMEM((8, rows, width), f32) for _ in range(4)],
        ),
        out_shape=jax.ShapeDtypeStruct((8, rows, 3 * part), bf16),
        compiler_params=pltpu.CompilerParams(vmem_limit_bytes=40 << 20),
        cost_estimate=cost(11.5),
        name="attention_back",
    )(slopes, qkv, qkv, qkv, d_ctx, lse)


def take(values, index, axis, size=1):
    starts = [0] * values.ndim
    starts[axis] = index
    sizes = list(values.shape)
    sizes[axis] = size
    return lax.dynamic_slice(values, starts, sizes)


def put(values, block, index, axis):
    starts = [0] * values.ndim
    starts[axis] = index
    return lax.dynamic_update_slice(values, block, starts)


def pick_kernel(info_ref, weight_ref, *refs, groups):
    outs, sems = refs[-NX - 1 : -1], refs[-1]
    rows, cols = outs[0].shape[0], outs[0].shape[1] // groups
    copies = []
    for k in range(NX):
        for group in range(groups):
            at = group * NX * 2 * cols + info_ref[1 + k] * cols
            copies.append(
                pltpu.make_async_copy(
                    weight_ref.at[
                        pl.ds(pl.multiple_of(info_ref[0] * rows, rows), rows),
                        pl.ds(pl.multiple_of(at, cols), cols),
                    ],
                    outs[k].at[:, pl.ds(group * cols, cols)],
                    sems.at[k * groups + group],
                )
            )
    for copy in copies:
        copy.start()
    for copy in copies:
        copy.wait()


def pick_columns(weight, groups, after):
    ax, az, core = lax.axis_index("x"), lax.axis_index("z"), lax.axis_index("c")
    rows, cols = weight.shape[0] // NZ, weight.shape[1] // (NX * 2)
    info = jnp.stack([az] + [(ax + k) % NX * 2 + core for k in range(NX)]).astype(jnp.int32)
    return pl.pallas_call(
        functools.partial(pick_kernel, groups=groups),
        grid_spec=pltpu.PrefetchScalarGridSpec(
            num_scalar_prefetch=1,
            grid=(1,),
            in_specs=[pl.BlockSpec(memory_space=pl.ANY)] * (1 + len(after)),
            out_specs=[pl.BlockSpec(memory_space=pl.ANY)] * NX,
            scratch_shapes=[pltpu.SemaphoreType.DMA((NX * groups,))],
        ),
        out_shape=[jax.ShapeDtypeStruct((rows, cols), weight.dtype)] * NX,
        compiler_params=kernel_params(),
        cost_estimate=cost(1.6),
        name="pick_columns",
    )(info, weight, *after)


def quarter_of_columns(weight, groups, after=()):
    ax, yh = lax.axis_index("x"), lax.axis_index("yh")
    pieces = pick_columns(weight, groups, after)
    by_x = jnp.zeros((NX,) + pieces[0].shape, bf16)
    for k in range(NX):
        got = pieces[k] if k == 0 else along_x(pieces[k], k)
        by_x = put(by_x, got[None], (ax - k) % NX, 0)
    other = along_y(by_x, 1, 1)
    by_xy = jnp.where(yh == 0, jnp.stack([by_x, other], 1), jnp.stack([other, by_x], 1))
    return by_xy.reshape((8,) + pieces[0].shape)


def assemble_kernel(info_ref, *refs):
    blocks, out_ref = refs[:NZ], refs[NZ]
    for k in range(NZ):
        out_ref[0, info_ref[k]] = blocks[k][0]


def assemble_planes(blocks):
    az = lax.axis_index("z")
    _, rows, cols = blocks[0].shape
    info = jnp.stack([(az - k) % NZ for k in range(NZ)]).astype(jnp.int32)
    full = pl.pallas_call(
        assemble_kernel,
        grid_spec=pltpu.PrefetchScalarGridSpec(
            num_scalar_prefetch=1,
            grid=(8,),
            in_specs=[pl.BlockSpec((1, rows, cols), lambda i, info: (i, 0, 0))] * NZ,
            out_specs=pl.BlockSpec((1, NZ, rows, cols), lambda i, info: (i, 0, 0, 0)),
        ),
        out_shape=jax.ShapeDtypeStruct((8, NZ, rows, cols), blocks[0].dtype),
        compiler_params=kernel_params(),
        cost_estimate=cost(4.0),
        name="assemble",
    )(info, *blocks)
    return full.reshape(8 * NZ * rows, cols)


def copy_kernel(source_ref, *refs):
    refs[-1][...] = source_ref[...]


def copy_after(values, after):
    rows, cols = values.shape
    spec = pl.BlockSpec((rows // 8, cols), lambda i: (i, 0))
    return pl.pallas_call(
        copy_kernel,
        grid=(8,),
        in_specs=[spec] + [pl.BlockSpec(memory_space=pl.ANY)] * len(after),
        out_specs=spec,
        out_shape=jax.ShapeDtypeStruct(values.shape, values.dtype),
        compiler_params=kernel_params(),
        cost_estimate=cost(4.0),
        name="copy_after",
    )(values, *after)


SLOTS = ("z", "yl", "yh")


def sum_kernel(pieces_ref, out_ref):
    out_ref[...] = jnp.sum(pieces_ref[...].astype(f32), axis=0).astype(out_ref.dtype)


def sum_over_slots(pieces, name, after=()):
    got = lax.all_to_all(pieces, SLOTS, 0, 0, tiled=True)
    if after:
        got = gate([got], list(after))[0]
    count, rows, cols = got.shape
    step = min(rows, 32)
    return pl.pallas_call(
        sum_kernel,
        grid=(rows // step,),
        in_specs=[pl.BlockSpec((count, step, cols), lambda i: (0, i, 0))],
        out_specs=pl.BlockSpec((step, cols), lambda i: (i, 0)),
        out_shape=jax.ShapeDtypeStruct((rows, cols), bf16),
        compiler_params=kernel_params(),
        cost_estimate=cost(3.0),
        name=name + "_sum",
    )(got)


def column_pieces(grad):
    part, cols = grad.shape[0] // (2 * NX), grad.shape[1]
    pieces = grad.reshape(NX, 2, 2, NZ, part // (2 * NZ), cols).transpose(3, 2, 1, 0, 4, 5)
    return pieces.reshape(16, NX * (part // (2 * NZ)), cols)


def row_planes(own):
    az, yl, yh, core = (lax.axis_index(n) for n in ("z", "yl", "yh", "c"))
    own = move(own)
    other = along_y(own, 1, 0)
    both = jnp.where(yl == 0, jnp.stack([own, other]), jnp.stack([other, own]))
    full = jnp.zeros((NZ,) + both.shape, both.dtype)
    for k in range(NZ):
        got = both if k == 0 else along_z(both, k)
        full = put(full, got[None], (az - k) % NZ, 0)
    theirs = across_core(full)
    out = jnp.where(core == 0, jnp.stack([full, theirs], 2), jnp.stack([theirs, full], 2))
    return out.reshape((8, 2) + own.shape)


def place_kernel(info_ref, *refs, groups):
    out_ref = refs[-1]
    core, step = info_ref[0], pl.program_id(0)
    for side in range(2):
        for k in range(NZ):
            ref = refs[side * NZ + k]

            @pl.when(step // 2 == k)
            def _(ref=ref, side=side):
                block = ref[step % 2]
                cols = block.shape[-1] // groups
                for group in range(groups):
                    for chip in range(NX):
                        at = (group * 2 * NX + chip * 2 + (core ^ side)) * cols
                        out_ref[:, pl.ds(pl.multiple_of(at, cols), cols)] = block[
                            chip, :, group * cols : (group + 1) * cols
                        ].astype(f32)


def place_planes(pieces, groups):
    az, yl, core = lax.axis_index("z"), lax.axis_index("yl"), lax.axis_index("c")
    _, _, rows, n = pieces[0].shape
    info = jnp.stack([core] + [(yl ^ i) * NZ + (az - k) % NZ for k in range(NZ) for i in range(2)])
    full = pl.BlockSpec(pieces[0].shape, lambda i, info: (0, 0, 0, 0))
    return pl.pallas_call(
        functools.partial(place_kernel, groups=groups),
        grid_spec=pltpu.PrefetchScalarGridSpec(
            num_scalar_prefetch=1,
            grid=(8,),
            in_specs=[full] * 8,
            out_specs=pl.BlockSpec((rows, 8 * n), lambda i, info: (info[1 + i], 0)),
        ),
        out_shape=jax.ShapeDtypeStruct((8 * rows, 8 * n), f32),
        compiler_params=kernel_params(),
        cost_estimate=cost(7.0),
        name="place_planes",
    )(info.astype(jnp.int32), *pieces)


def place_columns(own, groups):
    both = jnp.stack([own, along_y(own, 1, 0)])
    planes = [both] + [along_z(both, k) for k in (1, 2, 3)]
    return place_planes(planes + [across_core(p) for p in planes], groups)


def rows_of_member(sums):
    ax = lax.axis_index("x")
    out = jnp.zeros(sums.shape, sums.dtype)
    for k in range(NX):
        block = take(sums, (ax + k) % NX, 0)
        got = block if k == 0 else along_x(block, k)
        out = put(out, got, (ax - k) % NX, 0)
    return out


def local(tokens, lengths, vectors, fc1_bias, w_qkv, w_dense, w_fc1, w_fc2, cotangent):
    rows, width = tokens.shape
    ax, az = lax.axis_index("x"), lax.axis_index("z")
    core, yh = lax.axis_index("c"), lax.axis_index("yh")
    part = width // 8
    ff_part = fc1_bias.shape[0]
    heads = part // HEAD_DIM
    slot = rows * 8
    own_pos = jnp.arange(rows, dtype=jnp.int32) * 8 + ax * 2 + yh
    valid = (own_pos < lengths[0]).astype(f32)[:, None]

    tok = move(tokens)
    quarter_qkv, tok = gate([quarter_of_columns(w_qkv, 3), tok], [])
    tok_blocks = gather_rows(tok)

    packed = jnp.concatenate([vectors, fc1_bias.reshape(ff_part // part, part)])
    by_x = jnp.zeros((NX,) + packed.shape, f32)
    for k in range(NX):
        got = packed if k == 0 else along_x(packed, k)
        by_x = put(by_x, got[None], (ax - k) % NX, 0)
    other = along_y(by_x, 0, 1)
    packed = jnp.where(yh == 0, jnp.stack([by_x, other], 1), jnp.stack([other, by_x], 1))
    packed = packed.reshape(8, -1, part)
    vec_all = packed[:, :8].transpose(1, 0, 2).reshape(8, width)
    packed_part = take(packed, ax * 2 + core, 0)[0]
    vec_part, bias_part = packed_part[:8], packed_part[8:].reshape(ff_part)

    wq = lax.all_gather(quarter_qkv, "z", axis=1, tiled=True).reshape(width, 3 * part)
    quarter_fc1 = quarter_of_columns(w_fc1, 1, [quarter_qkv])
    wf1 = lax.all_gather(quarter_fc1, "z", axis=1, tiled=True).reshape(width, ff_part)
    wd = move(w_dense)
    rows_of = lambda n: jax.ShapeDtypeStruct((8, rows, n), bf16)
    dm_own = move((valid * cotangent.astype(f32)).astype(bf16))
    (dm,) = row_call(
        collect_kernel, gather_rows(dm_own), [], [], [rows_of(width)], "collect", 5.0
    )

    bias_qkv = jnp.concatenate([vec_part[2], jnp.zeros((part,), f32), vec_part[3]])
    (a_b,) = row_call(norm_kernel, tok_blocks, [vec_all], [], [rows_of(width)], "norm", 8.0)
    a_b, bias_qkv = gate([a_b, bias_qkv[None]], [quarter_fc1, wd, dm])
    qkv = project_qkv(a_b, wq, bias_qkv)

    head = ((ax * 2 + core) * heads + jnp.arange(heads, dtype=jnp.int32)).astype(f32)
    slopes = jnp.exp2(-8.0 * (head + 1.0) / (heads * 8))
    ctx, lse = attention(qkv, slopes)
    attn_terms = scatter_rows(ctx, wd, False, "dense")
    wf2 = move_late(copy_after(w_fc2, [quarter_fc1, vec_all, wd, dm]), [ctx])
    d_act = dot_t(dm.reshape(slot, width), wf2).astype(bf16).reshape(8, rows, ff_part)
    attn_terms = gate(attn_terms, [d_act])
    hidden = tok.astype(f32) + total(attn_terms) + vec_all[4]
    unit_two, inverse_two = normalize(hidden)
    c_own = (unit_two * vec_all[5] + vec_all[6]).astype(bf16)
    c_blocks = gather_rows(c_own)
    c_b, act_b, du_b, du_sum = row_call(
        mlp_kernel,
        c_blocks,
        [wf1, bias_part[None]],
        [d_act],
        [
            rows_of(width),
            rows_of(ff_part),
            rows_of(ff_part),
            jax.ShapeDtypeStruct((1, ff_part), f32),
        ],
        "feed_forward",
        13.7,
    )
    dc_chips = mine_part(
        du_b, wf1, theirs_part(du_b, wf1, True, "fc1_back"), True, "fc1_back"
    )
    dc_terms = send_chips(dc_chips)
    act_late, c_late = gate([act_b, c_b], [dc_chips[0]])
    g_fc2 = t_dot(act_late.reshape(slot, ff_part), dm.reshape(slot, width)).astype(bf16)
    g_fc1 = t_dot(c_late.reshape(slot, width), du_b.reshape(slot, ff_part)).astype(bf16)
    dc_terms = gate(dc_terms, [g_fc2, g_fc1])
    dc = total(dc_terms)
    dh = dm_own.astype(f32) + norm_back(dc, unit_two, inverse_two, vec_all[5])
    dh_own = dh.astype(bf16)
    dh_blocks = gather_rows(dh_own)
    dh_b, dctx = row_call(
        ctx_back_kernel, dh_blocks, [wd], [], [rows_of(width), rows_of(part)], "dense_back", 6.8
    )
    d_proj = attention_back(qkv, dctx, lse, slopes)
    g_qkv = t_dot(a_b.reshape(slot, width), d_proj.reshape(slot, 3 * part)).astype(bf16)
    d_proj_late, g_qkv = gate([d_proj, g_qkv], [])
    da_chips = mine_part(
        d_proj_late, wq, theirs_part(d_proj_late, wq, True, "qkv_back"), True, "qkv_back"
    )
    da_terms = send_chips(da_chips)
    act_late = gate([act_late], [da_chips[0]])[0]
    fc2_terms = scatter_rows(act_late, wf2, False, "fc2")
    g_dense = t_dot(ctx.reshape(slot, part), dh_b.reshape(slot, width)).astype(bf16)
    da = total(da_terms)
    own_unit, own_inverse = normalize(tok.astype(f32))
    d_tokens = move((dh + norm_back(da, own_unit, own_inverse, vec_all[0])).astype(bf16))
    d_proj = d_proj.reshape(slot, 3 * part)

    out_own = (hidden + total(fc2_terms) + vec_all[7]).astype(bf16)
    output = (valid * move(out_own).astype(f32)).astype(bf16)

    home = yh == core
    fc2_sum = sum_over_slots(g_fc2.reshape(16, ff_part // 16, width), "fc2")
    grad_fc2 = row_planes(fc2_sum).reshape(ff_part, width).astype(f32)
    fc1_sum = sum_over_slots(column_pieces(g_fc1), "fc1")
    fc1_sum = fc1_sum.reshape(NX, part // (2 * NZ), ff_part)
    grad_fc1 = place_columns(rows_of_member(fc1_sum), 1)
    qkv_sum = sum_over_slots(column_pieces(g_qkv), "qkv")
    qkv_sum = qkv_sum.reshape(NX, part // (2 * NZ), 3 * part)
    grad_qkv = place_columns(rows_of_member(qkv_sum), 3)

    token_terms = jnp.stack(
        [
            jnp.sum(da * own_unit, 0),
            jnp.sum(da, 0),
            jnp.sum(dh_own.astype(f32), 0),
            jnp.sum(dc * unit_two, 0),
            jnp.sum(dc, 0),
            jnp.sum(dm_own.astype(f32), 0),
        ]
    ).reshape(6, NX, 2, part)
    chip_terms = take(token_terms, core, 2) + across_core(take(token_terms, 1 - core, 2))
    chip_terms = chip_terms.reshape(6, NX, part)
    terms = take(chip_terms, ax, 1)
    for k in (1, 2, 3):
        terms = terms + along_x(take(chip_terms, (ax + k) % NX, 1), k)
    terms = jnp.concatenate(
        [
            terms[:, 0],
            jnp.sum(d_proj[:, :part].astype(f32), 0)[None],
            jnp.sum(d_proj[:, 2 * part :].astype(f32), 0)[None],
            du_sum.reshape(ff_part // part, part),
        ]
    ).astype(bf16)
    each = terms.size // 16
    terms = jnp.pad(terms.reshape(16, 1, each), ((0, 0), (0, 15), (0, width - each)))
    count = part // 16
    summed = sum_over_slots(
        jnp.concatenate([g_dense.reshape(16, count, width), terms], 1), "dense"
    )
    summed = row_planes(summed).reshape(16, count + 16, width).astype(f32)
    grad_dense = summed[:, :count].reshape(part, width)
    terms = summed[:, count, :each].reshape(12, part)
    grad_vectors = jnp.concatenate([terms[:2], terms[6:8], terms[2:6]])
    grad_bias = terms[8:].reshape(ff_part)
    return (output, d_tokens, grad_vectors, grad_bias, grad_qkv, grad_dense, grad_fc1, grad_fc2)


def solution(mesh):
    fine = Mesh(np.asarray(mesh.devices).reshape(4, 2, 2, 4, 2), ALL)
    rows = P(("z", "yl", "c", "x", "yh"), None)
    shard = P(("x", "yh"), None)
    return jax.shard_map(
        local,
        mesh=fine,
        in_specs=(
            rows,
            P(("z", "yl", "c")),
            P(None, ("x", "yh")),
            P(("x", "yh")),
            shard,
            shard,
            shard,
            shard,
            rows,
        ),
        out_specs=(
            rows,
            rows,
            P(None, ("x", "yh")),
            P(("x", "yh")),
            shard,
            shard,
            shard,
            shard,
        ),
        check_vma=False,
    )
```

```python
import functools

import numpy as np
import jax
import jax.numpy as jnp
from jax import lax
from jax.experimental import pallas as pl
from jax.experimental.pallas import tpu as pltpu
from jax.sharding import Mesh
from jax.sharding import PartitionSpec as P

HEAD_DIM = 64
EPSILON = 1e-05
bf16 = jnp.bfloat16
f32 = jnp.float32

ALL = ("z", "yl", "c", "x", "yh")
NX, NZ = 4, 4
SWAP = [(1, 2), (2, 1)]


def move(values):
    got = lax.ppermute(values, ("c", "yh"), SWAP)
    return jnp.where(lax.axis_index("c") == lax.axis_index("yh"), values, got)


def move_late(values, after):
    got = gate([lax.ppermute(values, ("c", "yh"), SWAP)], after)[0]
    return jnp.where(lax.axis_index("c") == lax.axis_index("yh"), values, got)


def across_core(values):
    return lax.ppermute(values, "c", [(0, 1), (1, 0)])


def along_x(values, step):
    return lax.ppermute(values, "x", [(i, (i + step) % NX) for i in range(NX)])


def along_z(values, step):
    return lax.ppermute(values, "z", [(i, (i + step) % NZ) for i in range(NZ)])


def along_y(values, flip_yl, flip_yh):
    pairs = [(i, i ^ (2 * flip_yl + flip_yh)) for i in range(4)]
    return lax.ppermute(values, ("yl", "yh"), pairs)


def gather_rows(block):
    mine = {0: block}
    for k in (1, 3, 2):
        mine[k] = along_x(block, k)
    theirs = {k: across_core(mine[k]) for k in (0, 1, 3, 2)}
    return [part[k] for k in range(NX) for part in (mine, theirs)]


def where_blocks():
    ax, core = lax.axis_index("x"), lax.axis_index("c")
    return jnp.stack(
        [(core ^ r) * NX + (ax - k) % NX for k in range(NX) for r in range(2)]
    ).astype(jnp.int32)


def gate(values, after):
    anywhere = pl.BlockSpec(memory_space=pl.ANY)
    out = pl.pallas_call(
        lambda *refs: None,
        in_specs=[anywhere] * (len(values) + len(after)),
        out_specs=[anywhere] * len(values),
        out_shape=[jax.ShapeDtypeStruct(v.shape, v.dtype) for v in values],
        input_output_aliases={i: i for i in range(len(values))},
        cost_estimate=cost(0),
        name="gate",
    )(*values, *after)
    return list(out)


def cost(us):
    return pl.CostEstimate(flops=int(us * 1e9), bytes_accessed=int(us * 3.2e6), transcendentals=0)


def kernel_params(mib=56):
    return pltpu.CompilerParams(vmem_limit_bytes=mib << 20)


def theirs_kernel(info_ref, left_ref, right_ref, out_ref, *, contract):
    rows = left_ref.shape[1]
    out_ref[...] = lax.dot_general(
        left_ref[...].reshape(NX * rows, left_ref.shape[2]),
        right_ref[...],
        contract,
        preferred_element_type=f32,
    ).astype(out_ref.dtype)


def mine_kernel(info_ref, left_ref, right_ref, got_ref, *refs, contract):
    outs, sum_ref = refs[:NX], refs[NX]
    rows = left_ref.shape[1]
    sum_ref[...] = lax.dot_general(
        left_ref[...].reshape(NX * rows, left_ref.shape[2]),
        right_ref[...],
        contract,
        preferred_element_type=f32,
    ) + got_ref[...].astype(f32)
    for k in range(NX):
        at = pl.ds(pl.multiple_of(info_ref[1 + k] * rows, rows), rows)
        outs[k][...] = sum_ref[at, :].astype(outs[k].dtype)


def group_info():
    ax, core = lax.axis_index("x"), lax.axis_index("c")
    return jnp.stack([core] + [(ax - k) % NX for k in range(NX)]).astype(jnp.int32)


def right_side(right, transposed, tile):
    if transposed:
        return right.shape[0], pl.BlockSpec((tile, right.shape[1]), lambda n, info: (n, 0))
    return right.shape[1], pl.BlockSpec((right.shape[0], tile), lambda n, info: (0, n))


def theirs_part(left, right, transposed, name, tile=512):
    rows, depth = left.shape[1:]
    width, right_spec = right_side(right, transposed, tile)
    contract = (((1,), (1 if transposed else 0,)), ((), ()))
    sent = pl.pallas_call(
        functools.partial(theirs_kernel, contract=contract),
        grid_spec=pltpu.PrefetchScalarGridSpec(
            num_scalar_prefetch=1,
            grid=(width // tile,),
            in_specs=[
                pl.BlockSpec((NX, rows, depth), lambda n, info: (1 - info[0], 0, 0)),
                right_spec,
            ],
            out_specs=pl.BlockSpec((NX * rows, tile), lambda n, info: (0, n)),
        ),
        out_shape=jax.ShapeDtypeStruct((NX * rows, width), bf16),
        compiler_params=kernel_params(),
        cost_estimate=cost(5.0 if depth < 512 else 6.5),
        name=name + "_theirs",
    )(group_info(), left, right)
    return across_core(sent)


def mine_part(left, right, got, transposed, name, tile=512):
    rows, depth = left.shape[1:]
    width, right_spec = right_side(right, transposed, tile)
    contract = (((1,), (1 if transposed else 0,)), ((), ()))
    return pl.pallas_call(
        functools.partial(mine_kernel, contract=contract),
        grid_spec=pltpu.PrefetchScalarGridSpec(
            num_scalar_prefetch=1,
            grid=(width // tile,),
            in_specs=[
                pl.BlockSpec((NX, rows, depth), lambda n, info: (info[0], 0, 0)),
                right_spec,
                pl.BlockSpec((NX * rows, tile), lambda n, info: (0, n)),
            ],
            out_specs=[pl.BlockSpec((rows, tile), lambda n, info: (0, n))] * NX,
            scratch_shapes=[pltpu.VMEM((NX * rows, tile), f32)],
        ),
        out_shape=[jax.ShapeDtypeStruct((rows, width), f32 if k == 0 else bf16) for k in range(NX)],
        compiler_params=kernel_params(),
        cost_estimate=cost(5.4 if depth < 512 else 7.0),
        name=name + "_mine",
    )(group_info(), left, right, got)


def send_chips(chips):
    return [chips[0]] + [along_x(chips[k], -k) for k in (2, 1, 3)]


def scatter_rows(left, right, transposed, name):
    got = theirs_part(left, right, transposed, name)
    return send_chips(mine_part(left, right, got, transposed, name))


def total(terms):
    result = terms[0]
    for term in terms[1:]:
        result = result + term.astype(f32)
    return result


def row_call(kernel, blocks, fixed, per_row, outs, name, us):
    whole = lambda v: pl.BlockSpec(v.shape, lambda i, at, nd=len(v.shape): (0,) * nd)
    return pl.pallas_call(
        kernel,
        grid_spec=pltpu.PrefetchScalarGridSpec(
            num_scalar_prefetch=1,
            grid=(1,),
            in_specs=[whole(v) for v in blocks + fixed + per_row],
            out_specs=[whole(v) for v in outs],
        ),
        out_shape=outs,
        compiler_params=kernel_params(),
        cost_estimate=cost(us),
        name=name,
    )(where_blocks(), *blocks, *fixed, *per_row)


def collect_kernel(at_ref, *refs):
    for i in range(8):
        refs[8][at_ref[i]] = refs[i][...]


def pair_of(refs, k):
    return jnp.concatenate([refs[2 * k][...], refs[2 * k + 1][...]], 0)


def put_pair(ref, at_ref, k, values):
    rows = ref.shape[1]
    for r in range(2):
        ref[at_ref[2 * k + r]] = values[r * rows : (r + 1) * rows]


def norm_kernel(at_ref, *refs):
    blocks, (gain_ref, a_ref) = refs[:8], refs[8:]
    for i in range(8):
        unit, _ = normalize(blocks[i][...].astype(f32))
        a_ref[at_ref[i]] = (unit * gain_ref[0:1, :] + gain_ref[1:2, :]).astype(bf16)


def qkv_kernel(a_ref, weight_ref, bias_ref, qkv_ref):
    blocks, rows, depth = a_ref.shape
    out = jnp.dot(
        a_ref[...].reshape(blocks * rows, depth), weight_ref[...], preferred_element_type=f32
    )
    qkv_ref[...] = (out + bias_ref[...]).astype(bf16).reshape(blocks, rows, out.shape[1])


def project_qkv(a_b, weight, bias):
    blocks, rows, depth = a_b.shape
    cols, step = weight.shape[1], 2
    return pl.pallas_call(
        qkv_kernel,
        grid=(blocks // step,),
        in_specs=[
            pl.BlockSpec((step, rows, depth), lambda i: (i, 0, 0)),
            pl.BlockSpec(weight.shape, lambda i: (0, 0)),
            pl.BlockSpec(bias.shape, lambda i: (0, 0)),
        ],
        out_specs=pl.BlockSpec((step, rows, cols), lambda i: (i, 0, 0)),
        out_shape=jax.ShapeDtypeStruct((blocks, rows, cols), bf16),
        compiler_params=kernel_params(),
        cost_estimate=cost(7.0),
        name="qkv",
    )(a_b, weight, bias)


def mlp_kernel(at_ref, *refs):
    blocks, (weight_ref, bias_ref, d_act_ref, c_ref, act_ref, du_ref, sum_ref) = refs[:8], refs[8:]
    sums = jnp.zeros(sum_ref.shape, f32)
    for k in range(NX):
        c = pair_of(blocks, k)
        put_pair(c_ref, at_ref, k, c)
        pre = jnp.dot(c, weight_ref[...], preferred_element_type=f32) + bias_ref[...]
        share = 0.5 + 0.5 * lax.erf(pre * (0.5**0.5))
        put_pair(act_ref, at_ref, k, (pre * share).astype(bf16))
        slope = share + pre * (jnp.exp(-0.5 * pre * pre) * ((2.0 * np.pi) ** -0.5))
        d_act = jnp.concatenate([d_act_ref[at_ref[2 * k]], d_act_ref[at_ref[2 * k + 1]]], 0)
        du = (d_act.astype(f32) * slope).astype(bf16)
        put_pair(du_ref, at_ref, k, du)
        sums = sums + jnp.sum(du.astype(f32), axis=0, keepdims=True)
    sum_ref[...] = sums


def ctx_back_kernel(at_ref, *refs):
    blocks, (weight_ref, dh_ref, out_ref) = refs[:8], refs[8:]
    for k in range(NX):
        dh = pair_of(blocks, k)
        put_pair(dh_ref, at_ref, k, dh)
        out = lax.dot_general(
            dh, weight_ref[...], (((1,), (1,)), ((), ())), preferred_element_type=f32
        )
        put_pair(out_ref, at_ref, k, out.astype(bf16))


def normalize(values):
    average = jnp.mean(values, axis=-1, keepdims=True)
    centred = values - average
    variance = jnp.mean(centred * centred, axis=-1, keepdims=True)
    inverse = lax.rsqrt(variance + EPSILON)
    return centred * inverse, inverse


def norm_back(grad_out, normed, inverse, gain_row):
    scaled = grad_out * gain_row
    inner = (
        scaled
        - jnp.mean(scaled, axis=-1, keepdims=True)
        - normed * jnp.mean(scaled * normed, axis=-1, keepdims=True)
    )
    return inner * inverse


def dot(left, right):
    return jnp.dot(left, right, preferred_element_type=f32)


def dot_t(left, right):
    return lax.dot_general(left, right, (((1,), (1,)), ((), ())), preferred_element_type=f32)


def t_dot(left, right):
    return lax.dot_general(left, right, (((0,), (0,)), ((), ())), preferred_element_type=f32)


TB = 32
MASKED = -1e30


def first_position(block):
    return block % NX * 2 + block // NX


def attention_setup(slope_ref, bias_ref, pos_ref, head):
    blocks, rows, lanes = pos_ref.shape
    slope = slope_ref[head]
    steps = lax.broadcasted_iota(jnp.int32, (rows, lanes), 0).astype(f32) * 8.0
    for block in range(blocks):
        at = steps + float(first_position(block))
        pos_ref[block] = at
        bias_ref[block] = at * slope
    return slope


def query_positions(start):
    lane = lax.broadcasted_iota(jnp.int32, (1, 8 * TB), 1)
    block, step = lane // TB, lane % TB
    return ((start + step) * 8 + first_position(block)).astype(f32)


def masked_scores(keys, queries, bias_ref, pos_ref, slope, i):
    count = 8 * TB * (i + 1)
    raw = lax.dot_general(
        keys, queries, (((1,), (1,)), ((), ())), preferred_element_type=f32
    )
    offset = slope * float(8 * TB * i)
    half = bias_ref.shape[2]
    bias = bias_ref[:, : TB * (i + 1), :].reshape(count, half) - offset
    pos = pos_ref[:, : TB * (i + 1), :].reshape(count, half)
    at = query_positions(TB * i)
    parts = [
        jnp.where(
            pos <= at[:, side * half : (side + 1) * half],
            raw[:, side * half : (side + 1) * half] + bias,
            MASKED,
        )
        for side in range(2)
    ]
    return jnp.concatenate(parts, 1)


def block_rows(ref, start, stop):
    return ref[:, start:stop, :].reshape(8 * (stop - start), ref.shape[2])


def attention_kernel(slope_ref, q_ref, k_ref, v_ref, ctx_ref, lse_ref, bias_ref, pos_ref):
    pair, side = pl.program_id(0), pl.program_id(1)
    slope = attention_setup(slope_ref, bias_ref, pos_ref, pair * 2 + side)
    lanes = lax.broadcasted_iota(jnp.int32, (1, 2 * HEAD_DIM), 1) // HEAD_DIM
    mine = lanes == side
    pick = mine.astype(bf16)
    for i in range(q_ref.shape[1] // TB):
        queries = block_rows(q_ref, TB * i, TB * (i + 1)) * (pick * (HEAD_DIM**-0.5))
        keys = block_rows(k_ref, 0, TB * (i + 1))
        values = block_rows(v_ref, 0, TB * (i + 1))
        s = masked_scores(keys, queries, bias_ref, pos_ref, slope, i)
        top = jnp.max(s, axis=0, keepdims=True)
        e = jnp.exp(s - top)
        total = jnp.sum(e, axis=0, keepdims=True)
        att = (e * (1.0 / total)).astype(bf16)
        ctx = lax.dot_general(
            values, att, (((0,), (0,)), ((), ())), preferred_element_type=f32
        ).T.reshape(8, TB, 2 * HEAD_DIM)
        before = ctx_ref[:, TB * i : TB * (i + 1), :]
        ctx_ref[:, TB * i : TB * (i + 1), :] = jnp.where(
            mine[:, None, :], ctx.astype(bf16), before
        )
        lse_ref[0, i : i + 1, :] = top + jnp.log(total)


def attention_back_kernel(
    slope_ref, q_ref, k_ref, v_ref, do_ref, lse_ref, out_ref, bias_ref, pos_ref, dk_ref, dv_ref
):
    pair, side = pl.program_id(0), pl.program_id(1)
    slope = attention_setup(slope_ref, bias_ref, pos_ref, pair * 2 + side)
    lanes = lax.broadcasted_iota(jnp.int32, (1, 2 * HEAD_DIM), 1) // HEAD_DIM
    mine = lanes == side
    pick = mine.astype(bf16)
    scale = HEAD_DIM**-0.5
    width = 2 * HEAD_DIM

    @pl.when(side == 0)
    def _():
        dk_ref[...] = jnp.zeros_like(dk_ref)
        dv_ref[...] = jnp.zeros_like(dv_ref)

    at_q = pl.ds(pl.multiple_of(pair * width, width), width)
    for i in range(q_ref.shape[1] // TB):
        queries = block_rows(q_ref, TB * i, TB * (i + 1)) * (pick * scale)
        grads = block_rows(do_ref, TB * i, TB * (i + 1)) * pick
        keys = block_rows(k_ref, 0, TB * (i + 1))
        values = block_rows(v_ref, 0, TB * (i + 1))
        s = masked_scores(keys, queries, bias_ref, pos_ref, slope, i)
        att = jnp.exp(s - lse_ref[0, i : i + 1, :])
        d_prob = lax.dot_general(
            values, grads, (((1,), (1,)), ((), ())), preferred_element_type=f32
        )
        inner = jnp.sum(att * d_prob, axis=0, keepdims=True)
        ds = (att * (d_prob - inner)).astype(bf16)
        shape = (8, TB * (i + 1), width)
        dv_ref[:, : TB * (i + 1), :] += jnp.dot(
            att.astype(bf16), grads, preferred_element_type=f32
        ).reshape(shape)
        dk_ref[:, : TB * (i + 1), :] += jnp.dot(
            ds, queries, preferred_element_type=f32
        ).reshape(shape)
        dq = lax.dot_general(
            keys, ds, (((0,), (0,)), ((), ())), preferred_element_type=f32
        ).T.reshape(8, TB, width)
        before = out_ref[:, TB * i : TB * (i + 1), at_q]
        out_ref[:, TB * i : TB * (i + 1), at_q] = jnp.where(
            mine[:, None, :], (dq * scale).astype(bf16), before
        )

    @pl.when(side == 1)
    def _():
        part = out_ref.shape[2] // 3
        at_k = pl.ds(pl.multiple_of(part + pair * width, width), width)
        at_v = pl.ds(pl.multiple_of(2 * part + pair * width, width), width)
        out_ref[:, :, at_k] = dk_ref[...].astype(bf16)
        out_ref[:, :, at_v] = dv_ref[...].astype(bf16)


def qkv_specs(rows, pairs):
    width = 2 * HEAD_DIM
    return [
        pl.BlockSpec((8, rows, width), lambda g, h, *_, first=first: (0, 0, first + g))
        for first in (0, pairs, 2 * pairs)
    ]


def attention(qkv, slopes):
    rows, part = qkv.shape[1], qkv.shape[2] // 3
    pairs, width = part // (2 * HEAD_DIM), 2 * HEAD_DIM
    return pl.pallas_call(
        attention_kernel,
        grid_spec=pltpu.PrefetchScalarGridSpec(
            num_scalar_prefetch=1,
            grid=(pairs, 2),
            in_specs=qkv_specs(rows, pairs),
            out_specs=[
                pl.BlockSpec((8, rows, width), lambda g, h, *_: (0, 0, g)),
                pl.BlockSpec((1, rows // TB, 8 * TB), lambda g, h, *_: (2 * g + h, 0, 0)),
            ],
            scratch_shapes=[
                pltpu.VMEM((8, rows, width), f32),
                pltpu.VMEM((8, rows, width), f32),
            ],
        ),
        out_shape=[
            jax.ShapeDtypeStruct((8, rows, part), bf16),
            jax.ShapeDtypeStruct((2 * pairs, rows // TB, 8 * TB), f32),
        ],
        compiler_params=pltpu.CompilerParams(vmem_limit_bytes=40 << 20),
        cost_estimate=cost(10.2),
        name="attention",
    )(slopes, qkv, qkv, qkv)


def attention_back(qkv, d_ctx, lse, slopes):
    rows, part = qkv.shape[1], qkv.shape[2] // 3
    pairs, width = part // (2 * HEAD_DIM), 2 * HEAD_DIM
    return pl.pallas_call(
        attention_back_kernel,
        grid_spec=pltpu.PrefetchScalarGridSpec(
            num_scalar_prefetch=1,
            grid=(pairs, 2),
            in_specs=qkv_specs(rows, pairs)
            + [
                pl.BlockSpec((8, rows, width), lambda g, h, *_: (0, 0, g)),
                pl.BlockSpec((1, rows // TB, 8 * TB), lambda g, h, *_: (2 * g + h, 0, 0)),
            ],
            out_specs=pl.BlockSpec((8, rows, 3 * part), lambda g, h, *_: (0, 0, 0)),
            scratch_shapes=[pltpu.VMEM((8, rows, width), f32) for _ in range(4)],
        ),
        out_shape=jax.ShapeDtypeStruct((8, rows, 3 * part), bf16),
        compiler_params=pltpu.CompilerParams(vmem_limit_bytes=40 << 20),
        cost_estimate=cost(11.5),
        name="attention_back",
    )(slopes, qkv, qkv, qkv, d_ctx, lse)


def take(values, index, axis, size=1):
    starts = [0] * values.ndim
    starts[axis] = index
    sizes = list(values.shape)
    sizes[axis] = size
    return lax.dynamic_slice(values, starts, sizes)


def put(values, block, index, axis):
    starts = [0] * values.ndim
    starts[axis] = index
    return lax.dynamic_update_slice(values, block, starts)


def pick_kernel(info_ref, weight_ref, *refs, groups):
    outs, sems = refs[-NX - 1 : -1], refs[-1]
    rows, cols = outs[0].shape[0], outs[0].shape[1] // groups
    copies = []
    for k in range(NX):
        for group in range(groups):
            at = group * NX * 2 * cols + info_ref[1 + k] * cols
            copies.append(
                pltpu.make_async_copy(
                    weight_ref.at[
                        pl.ds(pl.multiple_of(info_ref[0] * rows, rows), rows),
                        pl.ds(pl.multiple_of(at, cols), cols),
                    ],
                    outs[k].at[:, pl.ds(group * cols, cols)],
                    sems.at[k * groups + group],
                )
            )
    for copy in copies:
        copy.start()
    for copy in copies:
        copy.wait()


def pick_columns(weight, groups, after):
    ax, az, core = lax.axis_index("x"), lax.axis_index("z"), lax.axis_index("c")
    rows, cols = weight.shape[0] // NZ, weight.shape[1] // (NX * 2)
    info = jnp.stack([az] + [(ax + k) % NX * 2 + core for k in range(NX)]).astype(jnp.int32)
    return pl.pallas_call(
        functools.partial(pick_kernel, groups=groups),
        grid_spec=pltpu.PrefetchScalarGridSpec(
            num_scalar_prefetch=1,
            grid=(1,),
            in_specs=[pl.BlockSpec(memory_space=pl.ANY)] * (1 + len(after)),
            out_specs=[pl.BlockSpec(memory_space=pl.ANY)] * NX,
            scratch_shapes=[pltpu.SemaphoreType.DMA((NX * groups,))],
        ),
        out_shape=[jax.ShapeDtypeStruct((rows, cols), weight.dtype)] * NX,
        compiler_params=kernel_params(),
        cost_estimate=cost(1.6),
        name="pick_columns",
    )(info, weight, *after)


def quarter_of_columns(weight, groups, after=()):
    ax, yh = lax.axis_index("x"), lax.axis_index("yh")
    pieces = pick_columns(weight, groups, after)
    by_x = jnp.zeros((NX,) + pieces[0].shape, bf16)
    for k in range(NX):
        got = pieces[k] if k == 0 else along_x(pieces[k], k)
        by_x = put(by_x, got[None], (ax - k) % NX, 0)
    other = along_y(by_x, 1, 1)
    by_xy = jnp.where(yh == 0, jnp.stack([by_x, other], 1), jnp.stack([other, by_x], 1))
    return by_xy.reshape((8,) + pieces[0].shape)


def assemble_kernel(info_ref, *refs):
    blocks, out_ref = refs[:NZ], refs[NZ]
    for k in range(NZ):
        out_ref[0, info_ref[k]] = blocks[k][0]


def assemble_planes(blocks):
    az = lax.axis_index("z")
    _, rows, cols = blocks[0].shape
    info = jnp.stack([(az - k) % NZ for k in range(NZ)]).astype(jnp.int32)
    full = pl.pallas_call(
        assemble_kernel,
        grid_spec=pltpu.PrefetchScalarGridSpec(
            num_scalar_prefetch=1,
            grid=(8,),
            in_specs=[pl.BlockSpec((1, rows, cols), lambda i, info: (i, 0, 0))] * NZ,
            out_specs=pl.BlockSpec((1, NZ, rows, cols), lambda i, info: (i, 0, 0, 0)),
        ),
        out_shape=jax.ShapeDtypeStruct((8, NZ, rows, cols), blocks[0].dtype),
        compiler_params=kernel_params(),
        cost_estimate=cost(4.0),
        name="assemble",
    )(info, *blocks)
    return full.reshape(8 * NZ * rows, cols)


def copy_kernel(source_ref, *refs):
    refs[-1][...] = source_ref[...]


def copy_after(values, after):
    rows, cols = values.shape
    spec = pl.BlockSpec((rows // 8, cols), lambda i: (i, 0))
    return pl.pallas_call(
        copy_kernel,
        grid=(8,),
        in_specs=[spec] + [pl.BlockSpec(memory_space=pl.ANY)] * len(after),
        out_specs=spec,
        out_shape=jax.ShapeDtypeStruct(values.shape, values.dtype),
        compiler_params=kernel_params(),
        cost_estimate=cost(4.0),
        name="copy_after",
    )(values, *after)


SLOTS = ("z", "yl", "yh")


def sum_kernel(pieces_ref, out_ref):
    out_ref[...] = jnp.sum(pieces_ref[...].astype(f32), axis=0).astype(out_ref.dtype)


def sum_over_slots(pieces, name, after=()):
    got = lax.all_to_all(pieces, SLOTS, 0, 0, tiled=True)
    if after:
        got = gate([got], list(after))[0]
    count, rows, cols = got.shape
    step = min(rows, 32)
    return pl.pallas_call(
        sum_kernel,
        grid=(rows // step,),
        in_specs=[pl.BlockSpec((count, step, cols), lambda i: (0, i, 0))],
        out_specs=pl.BlockSpec((step, cols), lambda i: (i, 0)),
        out_shape=jax.ShapeDtypeStruct((rows, cols), bf16),
        compiler_params=kernel_params(),
        cost_estimate=cost(3.0),
        name=name + "_sum",
    )(got)


def column_pieces(grad):
    part, cols = grad.shape[0] // (2 * NX), grad.shape[1]
    pieces = grad.reshape(NX, 2, 2, NZ, part // (2 * NZ), cols).transpose(3, 2, 1, 0, 4, 5)
    return pieces.reshape(16, NX * (part // (2 * NZ)), cols)


def row_planes(own):
    az, yl, yh, core = (lax.axis_index(n) for n in ("z", "yl", "yh", "c"))
    own = move(own)
    other = along_y(own, 1, 0)
    both = jnp.where(yl == 0, jnp.stack([own, other]), jnp.stack([other, own]))
    full = jnp.zeros((NZ,) + both.shape, both.dtype)
    for k in range(NZ):
        got = both if k == 0 else along_z(both, k)
        full = put(full, got[None], (az - k) % NZ, 0)
    theirs = across_core(full)
    out = jnp.where(core == 0, jnp.stack([full, theirs], 2), jnp.stack([theirs, full], 2))
    return out.reshape((8, 2) + own.shape)


def place_kernel(info_ref, *refs, groups):
    out_ref = refs[-1]
    core, step = info_ref[0], pl.program_id(0)
    for side in range(2):
        for k in range(NZ):
            ref = refs[side * NZ + k]

            @pl.when(step // 2 == k)
            def _(ref=ref, side=side):
                block = ref[step % 2]
                cols = block.shape[-1] // groups
                for group in range(groups):
                    for chip in range(NX):
                        at = (group * 2 * NX + chip * 2 + (core ^ side)) * cols
                        out_ref[:, pl.ds(pl.multiple_of(at, cols), cols)] = block[
                            chip, :, group * cols : (group + 1) * cols
                        ].astype(f32)


def place_planes(pieces, groups):
    az, yl, core = lax.axis_index("z"), lax.axis_index("yl"), lax.axis_index("c")
    _, _, rows, n = pieces[0].shape
    info = jnp.stack([core] + [(yl ^ i) * NZ + (az - k) % NZ for k in range(NZ) for i in range(2)])
    full = pl.BlockSpec(pieces[0].shape, lambda i, info: (0, 0, 0, 0))
    return pl.pallas_call(
        functools.partial(place_kernel, groups=groups),
        grid_spec=pltpu.PrefetchScalarGridSpec(
            num_scalar_prefetch=1,
            grid=(8,),
            in_specs=[full] * 8,
            out_specs=pl.BlockSpec((rows, 8 * n), lambda i, info: (info[1 + i], 0)),
        ),
        out_shape=jax.ShapeDtypeStruct((8 * rows, 8 * n), f32),
        compiler_params=kernel_params(),
        cost_estimate=cost(7.0),
        name="place_planes",
    )(info.astype(jnp.int32), *pieces)


def place_columns(own, groups):
    both = jnp.stack([own, along_y(own, 1, 0)])
    planes = [both] + [along_z(both, k) for k in (1, 2, 3)]
    return place_planes(planes + [across_core(p) for p in planes], groups)


def rows_of_member(sums):
    ax = lax.axis_index("x")
    out = jnp.zeros(sums.shape, sums.dtype)
    for k in range(NX):
        block = take(sums, (ax + k) % NX, 0)
        got = block if k == 0 else along_x(block, k)
        out = put(out, got, (ax - k) % NX, 0)
    return out


def local(tokens, lengths, vectors, fc1_bias, w_qkv, w_dense, w_fc1, w_fc2, cotangent):
    rows, width = tokens.shape
    ax, az = lax.axis_index("x"), lax.axis_index("z")
    core, yh = lax.axis_index("c"), lax.axis_index("yh")
    part = width // 8
    ff_part = fc1_bias.shape[0]
    heads = part // HEAD_DIM
    slot = rows * 8
    own_pos = jnp.arange(rows, dtype=jnp.int32) * 8 + ax * 2 + yh
    valid = (own_pos < lengths[0]).astype(f32)[:, None]

    tok = move(tokens)
    quarter_qkv, tok = gate([quarter_of_columns(w_qkv, 3), tok], [])
    tok_blocks = gather_rows(tok)

    packed = jnp.concatenate([vectors, fc1_bias.reshape(ff_part // part, part)])
    by_x = jnp.zeros((NX,) + packed.shape, f32)
    for k in range(NX):
        got = packed if k == 0 else along_x(packed, k)
        by_x = put(by_x, got[None], (ax - k) % NX, 0)
    other = along_y(by_x, 0, 1)
    packed = jnp.where(yh == 0, jnp.stack([by_x, other], 1), jnp.stack([other, by_x], 1))
    packed = packed.reshape(8, -1, part)
    vec_all = packed[:, :8].transpose(1, 0, 2).reshape(8, width)
    packed_part = take(packed, ax * 2 + core, 0)[0]
    vec_part, bias_part = packed_part[:8], packed_part[8:].reshape(ff_part)

    wq = lax.all_gather(quarter_qkv, "z", axis=1, tiled=True).reshape(width, 3 * part)
    quarter_fc1 = quarter_of_columns(w_fc1, 1, [quarter_qkv])
    wf1 = lax.all_gather(quarter_fc1, "z", axis=1, tiled=True).reshape(width, ff_part)
    wd = move(w_dense)
    rows_of = lambda n: jax.ShapeDtypeStruct((8, rows, n), bf16)
    dm_own = move((valid * cotangent.astype(f32)).astype(bf16))
    dm_own = gate([dm_own], [quarter_qkv])[0]
    dm = lax.all_gather(dm_own, ("c", "x"), axis=0, tiled=True).reshape(8, rows, width)

    bias_qkv = jnp.concatenate([vec_part[2], jnp.zeros((part,), f32), vec_part[3]])
    (a_b,) = row_call(norm_kernel, tok_blocks, [vec_all], [], [rows_of(width)], "norm", 8.0)
    a_b, bias_qkv = gate([a_b, bias_qkv[None]], [quarter_fc1, wd])
    qkv = project_qkv(a_b, wq, bias_qkv)

    head = ((ax * 2 + core) * heads + jnp.arange(heads, dtype=jnp.int32)).astype(f32)
    slopes = jnp.exp2(-8.0 * (head + 1.0) / (heads * 8))
    ctx, lse = attention(qkv, slopes)
    attn_terms = scatter_rows(ctx, wd, False, "dense")
    wf2 = move_late(copy_after(w_fc2, [quarter_fc1, vec_all, wd]), [ctx])
    d_act = dot_t(dm.reshape(slot, width), wf2).astype(bf16).reshape(8, rows, ff_part)
    attn_terms = gate(attn_terms, [d_act])
    hidden = tok.astype(f32) + total(attn_terms) + vec_all[4]
    unit_two, inverse_two = normalize(hidden)
    c_own = (unit_two * vec_all[5] + vec_all[6]).astype(bf16)
    c_blocks = gather_rows(c_own)
    c_b, act_b, du_b, du_sum = row_call(
        mlp_kernel,
        c_blocks,
        [wf1, bias_part[None]],
        [d_act],
        [
            rows_of(width),
            rows_of(ff_part),
            rows_of(ff_part),
            jax.ShapeDtypeStruct((1, ff_part), f32),
        ],
        "feed_forward",
        13.7,
    )
    dc_chips = mine_part(
        du_b, wf1, theirs_part(du_b, wf1, True, "fc1_back"), True, "fc1_back"
    )
    dc_terms = send_chips(dc_chips)
    act_late, c_late = gate([act_b, c_b], [dc_chips[0]])
    g_fc2 = t_dot(act_late.reshape(slot, ff_part), dm.reshape(slot, width)).astype(bf16)
    g_fc1 = t_dot(c_late.reshape(slot, width), du_b.reshape(slot, ff_part)).astype(bf16)
    dc_terms = gate(dc_terms, [g_fc2, g_fc1])
    dc = total(dc_terms)
    dh = dm_own.astype(f32) + norm_back(dc, unit_two, inverse_two, vec_all[5])
    dh_own = dh.astype(bf16)
    dh_blocks = gather_rows(dh_own)
    dh_b, dctx = row_call(
        ctx_back_kernel, dh_blocks, [wd], [], [rows_of(width), rows_of(part)], "dense_back", 6.8
    )
    d_proj = attention_back(qkv, dctx, lse, slopes)
    g_qkv = t_dot(a_b.reshape(slot, width), d_proj.reshape(slot, 3 * part)).astype(bf16)
    d_proj_late, g_qkv = gate([d_proj, g_qkv], [])
    da_chips = mine_part(
        d_proj_late, wq, theirs_part(d_proj_late, wq, True, "qkv_back"), True, "qkv_back"
    )
    da_terms = send_chips(da_chips)
    act_late = gate([act_late], [da_chips[0]])[0]
    fc2_terms = scatter_rows(act_late, wf2, False, "fc2")
    g_dense = t_dot(ctx.reshape(slot, part), dh_b.reshape(slot, width)).astype(bf16)
    da = total(da_terms)
    own_unit, own_inverse = normalize(tok.astype(f32))
    d_tokens = move((dh + norm_back(da, own_unit, own_inverse, vec_all[0])).astype(bf16))
    d_proj = d_proj.reshape(slot, 3 * part)

    out_own = (hidden + total(fc2_terms) + vec_all[7]).astype(bf16)
    output = (valid * move(out_own).astype(f32)).astype(bf16)

    home = yh == core
    fc2_sum = sum_over_slots(g_fc2.reshape(16, ff_part // 16, width), "fc2")
    grad_fc2 = row_planes(fc2_sum).reshape(ff_part, width).astype(f32)
    fc1_sum = sum_over_slots(column_pieces(g_fc1), "fc1")
    fc1_sum = fc1_sum.reshape(NX, part // (2 * NZ), ff_part)
    grad_fc1 = place_columns(rows_of_member(fc1_sum), 1)
    qkv_sum = sum_over_slots(column_pieces(g_qkv), "qkv")
    qkv_sum = qkv_sum.reshape(NX, part // (2 * NZ), 3 * part)
    grad_qkv = place_columns(rows_of_member(qkv_sum), 3)

    token_terms = jnp.stack(
        [
            jnp.sum(da * own_unit, 0),
            jnp.sum(da, 0),
            jnp.sum(dh_own.astype(f32), 0),
            jnp.sum(dc * unit_two, 0),
            jnp.sum(dc, 0),
            jnp.sum(dm_own.astype(f32), 0),
        ]
    ).reshape(6, NX, 2, part)
    chip_terms = take(token_terms, core, 2) + across_core(take(token_terms, 1 - core, 2))
    chip_terms = chip_terms.reshape(6, NX, part)
    terms = take(chip_terms, ax, 1)
    for k in (1, 2, 3):
        terms = terms + along_x(take(chip_terms, (ax + k) % NX, 1), k)
    terms = jnp.concatenate(
        [
            terms[:, 0],
            jnp.sum(d_proj[:, :part].astype(f32), 0)[None],
            jnp.sum(d_proj[:, 2 * part :].astype(f32), 0)[None],
            du_sum.reshape(ff_part // part, part),
        ]
    ).astype(bf16)
    each = terms.size // 16
    terms = jnp.pad(terms.reshape(16, 1, each), ((0, 0), (0, 15), (0, width - each)))
    count = part // 16
    summed = sum_over_slots(
        jnp.concatenate([g_dense.reshape(16, count, width), terms], 1), "dense"
    )
    summed = row_planes(summed).reshape(16, count + 16, width).astype(f32)
    grad_dense = summed[:, :count].reshape(part, width)
    terms = summed[:, count, :each].reshape(12, part)
    grad_vectors = jnp.concatenate([terms[:2], terms[6:8], terms[2:6]])
    grad_bias = terms[8:].reshape(ff_part)
    return (output, d_tokens, grad_vectors, grad_bias, grad_qkv, grad_dense, grad_fc1, grad_fc2)


def solution(mesh):
    fine = Mesh(np.asarray(mesh.devices).reshape(4, 2, 2, 4, 2), ALL)
    rows = P(("z", "yl", "c", "x", "yh"), None)
    shard = P(("x", "yh"), None)
    return jax.shard_map(
        local,
        mesh=fine,
        in_specs=(
            rows,
            P(("z", "yl", "c")),
            P(None, ("x", "yh")),
            P(("x", "yh")),
            shard,
            shard,
            shard,
            shard,
            rows,
        ),
        out_specs=(
            rows,
            rows,
            P(None, ("x", "yh")),
            P(("x", "yh")),
            shard,
            shard,
            shard,
            shard,
        ),
        check_vma=False,
    )
```
